32 devices in a mesh: dp: 8 (over z, x), tensor: 4 (over y, core).
Axes of the slice: x: 2, y: 2, z: 4, core: 2. Of those that a mesh axis runs over, the one named last changes fastest.
Arguments:
- block_input: float32 [8192, 1536], P('dp'), may hold values from -6 to 6
- segments: int32 [8, 1024], P('dp'), may hold values from 0 to 3, never falling along the last dimension, each value on 1 to 512 neighbouring positions
- routes: int32 [8192, 4], P('dp'), may hold values from 0 to 7, all different within a row
- gates: float32 [8192, 4], P('dp'), may hold values from 0.1 to 0.4
- cotangent: float32 [8192, 1536], P('dp'), may hold values from -6 to 6
- w_query: float32 [1536, 1536], P('dp', 'tensor'), may hold values from -0.15625 to 0.15625
- m_query: float32 [1536, 1536], P('dp', 'tensor'), may hold values from -16 to 16
- v_query: float32 [1536, 1536], P('dp', 'tensor'), may hold values from 40.96 to 163.84
- w_keyval: float32 [1536, 2, 256], P(('dp', 'tensor')), may hold values from -0.15625 to 0.15625
- m_keyval: float32 [1536, 2, 256], P(('dp', 'tensor')), may hold values from -56 to 56
- v_keyval: float32 [1536, 2, 256], P(('dp', 'tensor')), may hold values from 409.6 to 1638.4
- w_output: float32 [1536, 1536], P('tensor', 'dp'), may hold values from -0.625 to 0.625
- m_output: float32 [1536, 1536], P('tensor', 'dp'), may hold values from -28 to 28
- v_output: float32 [1536, 1536], P('tensor', 'dp'), may hold values from 90.112 to 360.448
- w_gate_up: float32 [1536, 2, 8, 768], P('dp', None, None, 'tensor'), may hold values from -0.15625 to 0.15625
- m_gate_up: float32 [1536, 2, 8, 768], P('dp', None, None, 'tensor'), may hold values from -20 to 20
- v_gate_up: float32 [1536, 2, 8, 768], P('dp', None, None, 'tensor'), may hold values from 53.248 to 212.992
- w_down: float32 [8, 768, 1536], P(None, 'tensor', 'dp'), may hold values from -0.625 to 0.625
- m_down: float32 [8, 768, 1536], P(None, 'tensor', 'dp'), may hold values from -5 to 5
- v_down: float32 [8, 768, 1536], P(None, 'tensor', 'dp'), may hold values from 3.2768 to 13.9264
- gains: float32 [2, 1536], P(None, ('dp', 'tensor')), may hold values from 0.5 to 1.5
- m_gains: float32 [2, 1536], P(None, ('dp', 'tensor')), may hold values from -64 to 64
- v_gains: float32 [2, 1536], P(None, ('dp', 'tensor')), may hold values from 409.6 to 1638.4
Outputs:
- block_output: float32 [8192, 1536], P('dp')
- input_grad: float32 [8192, 1536], P('dp')
- new_w_query: float32 [1536, 1536], P('dp', 'tensor')
- new_m_query: float32 [1536, 1536], P('dp', 'tensor')
- new_v_query: float32 [1536, 1536], P('dp', 'tensor')
- new_w_keyval: float32 [1536, 2, 256], P(('dp', 'tensor'))
- new_m_keyval: float32 [1536, 2, 256], P(('dp', 'tensor'))
- new_v_keyval: float32 [1536, 2, 256], P(('dp', 'tensor'))
- new_w_output: float32 [1536, 1536], P('tensor', 'dp')
- new_m_output: float32 [1536, 1536], P('tensor', 'dp')
- new_v_output: float32 [1536, 1536], P('tensor', 'dp')
- new_w_gate_up: float32 [1536, 2, 8, 768], P('dp', None, None, 'tensor')
- new_m_gate_up: float32 [1536, 2, 8, 768], P('dp', None, None, 'tensor')
- new_v_gate_up: float32 [1536, 2, 8, 768], P('dp', None, None, 'tensor')
- new_w_down: float32 [8, 768, 1536], P(None, 'tensor', 'dp')
- new_m_down: float32 [8, 768, 1536], P(None, 'tensor', 'dp')
- new_v_down: float32 [8, 768, 1536], P(None, 'tensor', 'dp')
- new_gains: float32 [2, 1536], P(None, ('dp', 'tensor'))
- new_m_gains: float32 [2, 1536], P(None, ('dp', 'tensor'))
- new_v_gains: float32 [2, 1536], P(None, ('dp', 'tensor'))
The draws below stay inside these ranges and needn't reach their ends.
Inputs may be any that keep to these rules, and one draw needn't show every extreme that they name: `segments`: numbers start at 0 in every sequence, never fall, and all of 0 to 3 occur; one document of each sequence is 512 tokens long. `routes`: each token names 4 different experts; every expert is named by some token.
All inputs are finite; a program needn't handle non-finite values.
Results may differ from the reference program's by a relative error of at most 0.015.
Values may be sent and summed in bfloat16 or wider, within the bound.
No kernel may reach another device: no remote copies, remote signals or barrier semaphores. Data moves between devices by JAX's collectives and lax.ppermute only.
A program may use at most 256 MiB of HBM per device.

```python
import math
import jax
import jax.numpy as jnp
import numpy as np
from jax import lax

D = 1536
H = 12
KVH = 2
HD = 128
FF = 768
TOP = 4
E = 8
SEQ = 1024
STEP = 10
SEQS = 8
TOKENS = 8192
N_TENSOR = 4


def steps_of(own_key, extent, shards, least, top_value):
    factor_of = 1.0
    for dim, shards_of in shards:
        draws = jax.random.uniform(jax.random.fold_in(jax.random.fold_in(own_key, 6), dim), (shards_of,), jnp.float32, least / len(shards), top_value / len(shards))
        factor_of = factor_of * jnp.repeat(jnp.exp(draws), extent[dim] // shards_of).reshape((-1,) + (1,) * (len(extent) - 1 - dim))
    return factor_of


def picks_of(key, rows, amount, top, lift):
    order = jax.random.permutation(jax.random.fold_in(key, 1), amount)
    boost = order
    for power in range(3):
        boost = boost * boost // amount
    boost = boost * lift // amount
    tickets = jax.random.randint(jax.random.fold_in(key, 2), (rows, amount), 0, 4096) + boost
    fixed_rows = jax.random.permutation(jax.random.fold_in(key, 3), rows)[jnp.arange(amount) % rows]
    tickets = jnp.where(jnp.arange(rows)[:, None] == fixed_rows[None, :], 1 << 14, tickets)
    priority = tickets * amount + jnp.arange(amount)
    return lax.top_k(priority.astype(jnp.int32), top)[1].astype(jnp.int32)


def length_profile(amount, total, bound, slope):
    weights = [(1 << 20) // math.isqrt(grade ** slope) + 1 for grade in range(2, amount + 1)]
    rest, counts = total - bound - (amount - 1), [1] * (amount - 1)
    while rest > 0:
        movable = [i for i in range(amount - 1) if counts[i] < bound]
        whole, left = sum([weights[i] for i in movable]), rest
        for i in movable:
            addition = min(bound - counts[i], max(1, left * weights[i] // whole), rest)
            counts[i] = counts[i] + addition
            rest = rest - addition
    return np.array([bound] + counts)


def uneven(rng, number_of, total, bound, lean):
    if number_of == 2:
        one = jax.random.randint(rng, (), max(1, total - bound), min(bound, total - 1) + 1)
        return jnp.stack([one, total - one])
    tallies = jnp.asarray(length_profile(number_of, total, bound, lean), jnp.int32)
    twos = (number_of - 1) // 2
    source_of, receiver = tallies[1:1 + 2 * twos:2], tallies[2:2 + 2 * twos:2]
    slack = jnp.minimum(source_of - 1, bound - receiver)
    shifted = jax.random.randint(jax.random.fold_in(rng, 1), (twos,), 0, 1 << 20) % (slack + 1)
    tallies = tallies.at[1:1 + 2 * twos:2].set(source_of - shifted).at[2:2 + 2 * twos:2].set(receiver + shifted)
    return tallies[jax.random.permutation(jax.random.fold_in(rng, 2), number_of)]


def normal_values(rng, shape, width, bound, shards=(), dtype=jnp.bfloat16):
    array = jax.random.normal(rng, shape, jnp.float32) * width
    if len(shards) > 0:
        array = steps_of(rng, shape, shards, -0.22, 0.18) * array
    return jnp.clip(array, min=-bound, max=bound).astype(dtype)


def setup_inputs(seed: int = 0) -> dict:
    seeds = jax.random.split(jax.random.key(seed), 24)
    return {
        "block_input": normal_values(seeds[0], (TOKENS, D), 1.0, 6.0, ((0, 8),), jnp.float32),
        "segments": jax.vmap(lambda own: jnp.searchsorted(jnp.cumsum(uneven(own, 4, SEQ, SEQ // 2, 0)), jnp.arange(SEQ), side="right"))(jax.random.split(seeds[1], SEQS)).reshape((SEQS, SEQ)).astype(jnp.int32),
        "routes": picks_of(seeds[2], TOKENS, E, TOP, 4096),
        "gates": jnp.clip(0.1 + 0.3 * jax.random.uniform(seeds[3], (TOKENS, TOP), jnp.float32) ** steps_of(seeds[3], (TOKENS, TOP), ((0, 8),), -0.2, 0.2), 0.1, 0.4),
        "cotangent": normal_values(seeds[4], (TOKENS, D), 1.0, 6.0, ((0, 8),), jnp.float32),
        "w_query": normal_values(seeds[5], (D, H * HD), D ** -0.5, 0.15625, ((0, 8), (1, 4)), jnp.float32),
        "m_query": normal_values(seeds[6], (D, H * HD), (0.033 * TOKENS ** 0.5), 16.0, ((0, 8), (1, 4)), jnp.float32),
        "v_query": jnp.clip(jnp.exp(math.log(163.84) - 1.3862944 * jax.random.uniform(seeds[7], (D, H * HD), jnp.float32) ** steps_of(seeds[7], (D, H * HD), ((0, 8), (1, 4)), -0.2, 0.2)), 40.96, 163.84),
        "w_keyval": normal_values(seeds[8], (D, 2, KVH * HD), D ** -0.5, 0.15625, ((0, 32),), jnp.float32),
        "m_keyval": normal_values(seeds[9], (D, 2, KVH * HD), (0.1 * TOKENS ** 0.5), 56.0, ((0, 32),), jnp.float32),
        "v_keyval": jnp.clip(jnp.exp(math.log(1638.4) - 1.3862944 * jax.random.uniform(seeds[10], (D, 2, KVH * HD), jnp.float32) ** steps_of(seeds[10], (D, 2, KVH * HD), ((0, 32),), -0.2, 0.2)), 409.6, 1638.4),
        "w_output": normal_values(seeds[11], (H * HD, D), (H * HD // 16) ** -0.5, 0.625, ((0, 4), (1, 8)), jnp.float32),
        "m_output": normal_values(seeds[12], (H * HD, D), (0.05 * TOKENS ** 0.5), 28.0, ((0, 4), (1, 8)), jnp.float32),
        "v_output": jnp.clip(jnp.exp(math.log(360.448) - 1.3862944 * jax.random.uniform(seeds[13], (H * HD, D), jnp.float32) ** steps_of(seeds[13], (H * HD, D), ((0, 4), (1, 8)), -0.2, 0.2)), 90.112, 360.448),
        "w_gate_up": normal_values(seeds[14], (D, 2, E, FF), D ** -0.5, 0.15625, ((0, 8), (3, 4)), jnp.float32),
        "m_gate_up": normal_values(seeds[15], (D, 2, E, FF), (0.04 * TOKENS ** 0.5), 20.0, ((0, 8), (3, 4)), jnp.float32),
        "v_gate_up": jnp.clip(jnp.exp(math.log(212.992) - 1.3862944 * jax.random.uniform(seeds[16], (D, 2, E, FF), jnp.float32) ** steps_of(seeds[16], (D, 2, E, FF), ((0, 8), (3, 4)), -0.2, 0.2)), 53.248, 212.992),
        "w_down": normal_values(seeds[17], (E, FF, D), (FF // 8) ** -0.5, 0.625, ((1, 4), (2, 8)), jnp.float32),
        "m_down": normal_values(seeds[18], (E, FF, D), (0.01 * TOKENS ** 0.5), 5.0, ((1, 4), (2, 8)), jnp.float32),
        "v_down": jnp.clip(jnp.exp(math.log(13.9264) - 1.446919 * jax.random.uniform(seeds[19], (E, FF, D), jnp.float32) ** steps_of(seeds[19], (E, FF, D), ((1, 4), (2, 8)), -0.2, 0.2)), 3.2768, 13.9264),
        "gains": jnp.clip(1.0 + 0.1 * jax.random.normal(seeds[20], (2, D), jnp.float32), 0.5, 1.5),
        "m_gains": normal_values(seeds[21], (2, D), (0.11 * TOKENS ** 0.5), 64.0, ((1, 32),), jnp.float32),
        "v_gains": jnp.clip(jnp.exp(math.log(1638.4) - 1.3862944 * jax.random.uniform(seeds[22], (2, D), jnp.float32) ** steps_of(seeds[22], (2, D), ((1, 32),), -0.2, 0.2)), 409.6, 1638.4),
    }


@jax.custom_vjp
def low(v):
    return lax.optimization_barrier(v.astype(jnp.bfloat16)).astype(jnp.float32)

@jax.custom_vjp
def low_back(v):
    return v

def low_keep(v):
    return (low(v), None)

def low_pass(kept, grad):
    return (grad,)

def back_keep(v):
    return (v, None)

def back_low(kept, grad):
    return (low(grad),)
low.defvjp(low_keep, low_pass)
low_back.defvjp(back_keep, back_low)
highest = lax.Precision.HIGHEST
norm_eps = 1e-06
beta_one = 0.9
beta_two = 0.95
adam_eps = 1e-08

def matmul(left, right):
    return jnp.dot(left, right, precision=highest, preferred_element_type=jnp.float32)

def rms_norm(rows, gain):
    return rows * lax.rsqrt(lax.optimization_barrier(jnp.mean(rows * rows, axis=-1, keepdims=True)) + norm_eps) * gain

def layer_rows(weights, rows, segment, route, gate):
    query_mat, keyval_mat, output_mat, gate_up_mat, down_mat, gain_rows = weights
    first = low(rms_norm(rows, gain_rows[0]))
    queries = low(low_back(matmul(first, query_mat))).reshape(SEQ, H, HD)
    per_group = H // N_TENSOR
    group_size = H // KVH
    copies = []
    for group in range(N_TENSOR):
        head = group * per_group // group_size
        columns = keyval_mat[:, :, head * HD:(head + 1) * HD].reshape(D, 2 * HD)
        copies.append(low(low_back(matmul(first, columns))).reshape(SEQ, 2, HD))
    keyvals = jnp.repeat(jnp.stack(copies), per_group, axis=0)
    keys = keyvals[:, :, 0]
    values = keyvals[:, :, 1]
    scores = jnp.einsum('qhd,hkd->hqk', queries, keys, precision=highest) * HD ** (-0.5)
    scores = low_back(scores)
    positions = jnp.arange(SEQ)
    allowed = (positions[:, None] >= positions[None, :]) & (segment[:, None] == segment[None, :])
    scores = jnp.where(allowed[None], scores, -1e+30)
    probs = low(jax.nn.softmax(scores, axis=-1))
    attended = jnp.einsum('hqk,hkd->qhd', probs, values, precision=highest).reshape(SEQ, H * HD)
    attended = low(low_back(attended))
    middle = rows + low_back(matmul(attended, output_mat))
    second = low(rms_norm(middle, gain_rows[1]))
    gate_up = low_back(matmul(second, gate_up_mat.reshape(D, 2 * E * FF))).reshape(SEQ, 2, E, FF)
    combine = lax.optimization_barrier(jnp.sum(gate[:, :, None] * (route[:, :, None] == jnp.arange(E)[None, None, :]).astype(jnp.float32), axis=1))
    hidden = low(combine[:, :, None] * jax.nn.gelu(gate_up[:, 0], approximate=True) * gate_up[:, 1])
    expert_out = matmul(hidden.reshape(SEQ, E * FF), down_mat.reshape(E * FF, D))
    return middle + low_back(expert_out)

def adam_step(weight, first_m, second_m, grad, rate, decay):
    new_m = beta_one * first_m + (1.0 - beta_one) * grad
    new_v = beta_two * second_m + (1.0 - beta_two) * grad * grad
    m_hat = new_m / (1.0 - beta_one ** STEP)
    v_hat = new_v / (1.0 - beta_two ** STEP)
    new_w = weight - rate * (m_hat / (jnp.sqrt(v_hat) + adam_eps) + decay * weight)
    return (new_w, new_m, new_v)

def reference(block_input, segments, routes, gates, cotangent, w_query, m_query, v_query, w_keyval, m_keyval, v_keyval, w_output, m_output, v_output, w_gate_up, m_gate_up, v_gate_up, w_down, m_down, v_down, gains, m_gains, v_gains):

    def forward(query_mat, keyval_mat, output_mat, gate_up_mat, down_mat, gain_rows, rows_all):
        weights = (low(query_mat), low(keyval_mat), low(output_mat), low(gate_up_mat), low(down_mat), gain_rows)

        def one_sequence(item):
            rows, segment, route, gate = item
            return layer_rows(weights, rows, segment, route, gate)
        outputs = lax.map(jax.checkpoint(one_sequence), (rows_all.reshape(SEQS, SEQ, D), segments, routes.reshape(SEQS, SEQ, TOP), gates.reshape(SEQS, SEQ, TOP)))
        return outputs.reshape(TOKENS, D)
    block_output, pullback = jax.vjp(forward, w_query, w_keyval, w_output, w_gate_up, w_down, gains, block_input)
    grads = pullback(cotangent)
    d_query, d_keyval, d_output, d_gate_up, d_down, d_gains, input_grad = grads
    query_new = adam_step(w_query, m_query, v_query, d_query, 0.05, 0.1)
    keyval_new = adam_step(w_keyval, m_keyval, v_keyval, d_keyval, 0.05, 0.1)
    output_new = adam_step(w_output, m_output, v_output, d_output, 0.05, 0.1)
    gate_up_new = adam_step(w_gate_up, m_gate_up, v_gate_up, d_gate_up, 0.05, 0.1)
    down_new = adam_step(w_down, m_down, v_down, d_down, 0.05, 0.1)
    gains_new = adam_step(gains, m_gains, v_gains, d_gains, 0.5, 0.0)
    return (block_output, input_grad, query_new[0], query_new[1], query_new[2], keyval_new[0], keyval_new[1], keyval_new[2], output_new[0], output_new[1], output_new[2], gate_up_new[0], gate_up_new[1], gate_up_new[2], down_new[0], down_new[1], down_new[2], gains_new[0], gains_new[1], gains_new[2])
```

```python
import math
from functools import partial

import jax
import jax.numpy as jnp
from jax import lax
from jax.experimental import pallas as pl
from jax.experimental.pallas import tpu as pltpu
from jax.sharding import PartitionSpec as P

H = 12
KVH = 2
HD = 128
E = 8
STEP = 10


norm_eps = 1e-06
beta_one = 0.9
beta_two = 0.95
adam_eps = 1e-08

bf = jnp.bfloat16
f32 = jnp.float32


def product(left, right):
    return jnp.dot(left, right, preferred_element_type=f32)


def against_rows(left, right):
    return lax.dot_general(left, right, (((1,), (1,)), ((), ())), preferred_element_type=f32)


def over_rows(left, right):
    return lax.dot_general(left, right, (((0,), (0,)), ((), ())), preferred_element_type=f32)


def adam_step(weight, first_m, second_m, grad, rate, decay):
    new_m = beta_one * first_m + (1.0 - beta_one) * grad
    new_v = beta_two * second_m + (1.0 - beta_two) * grad * grad
    m_hat = new_m / (1.0 - beta_one**STEP)
    v_hat = new_v / (1.0 - beta_two**STEP)
    new_w = weight - rate * (m_hat / (jnp.sqrt(v_hat) + adam_eps) + decay * weight)
    return (new_w, new_m, new_v)


ORDER = []
TOKEN = jax.ShapeDtypeStruct((8, 128), f32)


def call(kernel, outs, ins, in_specs, out_specs, grid=(), prefetch=0, scratch=(), aliases=None, ordered=True):
    tokens = tuple(ORDER) if ordered else ()
    several = isinstance(outs, tuple)
    outs = outs if several else (outs,)
    out_specs = out_specs if several else (out_specs,)
    first_out = len(ins) + len(tokens)
    last_out = first_out + len(outs)

    def ordered_kernel(*refs):
        kernel(*refs[: len(ins)], *refs[first_out:last_out], *refs[last_out + 1 :])

    results = pl.pallas_call(
        ordered_kernel,
        out_shape=(*outs, TOKEN),
        grid_spec=pltpu.PrefetchScalarGridSpec(
            num_scalar_prefetch=prefetch,
            grid=grid,
            in_specs=list(in_specs) + anywhere(len(tokens)),
            out_specs=(*out_specs, anywhere(1)[0]),
            scratch_shapes=scratch,
        ),
        input_output_aliases=aliases or {},
        cost_estimate=pl.CostEstimate(flops=1, bytes_accessed=1, transcendentals=0),
        compiler_params=pltpu.CompilerParams(vmem_limit_bytes=64 * 2**20),
    )(*ins, *tokens)
    if ordered:
        ORDER[:] = [results[-1]]
    return results[:-1] if several else results[0]


def anywhere(count):
    return [pl.BlockSpec(memory_space=pl.ANY)] * count


def nothing(*refs):
    pass


def after(*values):
    return call(
        nothing,
        tuple(jax.ShapeDtypeStruct(v.shape, v.dtype) for v in values),
        values,
        anywhere(len(values)),
        tuple(anywhere(len(values))),
        aliases={i: i for i in range(len(values))},
    )


def unwritten(shape, dtype):
    return call(nothing, jax.ShapeDtypeStruct(shape, dtype), (), [], anywhere(1)[0], ordered=False)


def put_kernel(extra, at_ref, *refs):
    buffers = 2 if extra else 1
    outs = refs[buffers + 2 :]
    rows = outs[0].shape[0]
    for step, ref in enumerate(refs[buffers : buffers + 2]):

        @pl.when(pl.program_id(0) == step)
        def _():
            outs[0][...] = ref[:rows]
            if extra:
                outs[1][...] = ref[rows:]


def put(buffers, low, high, rows, extra, at):
    places = jnp.stack([jnp.asarray(p, jnp.int32) for p in at])
    high = low if high is None else high
    columns = low.shape[1]
    specs = [pl.BlockSpec((size, columns), lambda i, at: (at[i], 0)) for size in (rows, extra) if size]
    return call(
        partial(put_kernel, extra),
        tuple(jax.ShapeDtypeStruct(b.shape, b.dtype) for b in buffers),
        (places, *buffers, low, high),
        anywhere(len(buffers))
        + [pl.BlockSpec(v.shape, lambda i, at: (0, 0)) for v in (low, high)],
        tuple(specs),
        grid=(len(at),),
        prefetch=1,
        aliases={1 + i: i for i in range(len(buffers))},
    )


def inverse_norm(rows):
    return lax.rsqrt(jnp.mean(rows * rows, axis=-1, keepdims=True) + norm_eps)


def row_blocks(rows):
    return min(256, rows // 4)


def norm_kernel(rows_ref, gain_ref, mat_ref, low_ref, qkv_ref):
    rows = rows_ref[...]
    low = (rows * inverse_norm(rows) * gain_ref[...]).astype(bf)
    low_ref[...] = low
    qkv_ref[...] = product(low, mat_ref[:, : qkv_ref.shape[1]]).astype(bf)


def norm_and_project(rows, gain, mat, columns):
    count, width = rows.shape
    block = row_blocks(count)
    by_rows = pl.BlockSpec((block, width), lambda i: (i, 0))
    whole = pl.BlockSpec((1, width), lambda i: (0, 0))
    return call(
        norm_kernel,
        (jax.ShapeDtypeStruct(rows.shape, bf), jax.ShapeDtypeStruct((count, columns), bf)),
        (rows, gain[None], mat),
        [by_rows, whole, pl.BlockSpec(mat.shape, lambda i: (0, 0))],
        (by_rows, pl.BlockSpec((block, columns), lambda i: (i, 0))),
        grid=(count // block,),
    )


PIECES = 2


def piece_specs(count, width, block):
    half = count // (2 * block)
    size = half // PIECES

    def spec(own, piece):
        def place(i, side):
            first = (side[0] if own else 1 - side[0]) * half + piece * size
            return (jnp.clip(i - first, 0, size - 1), 0)

        return pl.BlockSpec((block, width), place)

    return [spec(own, piece) for piece in range(PIECES) for own in (True, False)]


def pick_piece(side_ref, refs, value_ref):
    step, half = pl.program_id(0), pl.num_programs(0) // 2
    own = (step // half) == side_ref[0]
    at = (step % half) // (half // PIECES)
    for piece in range(PIECES):
        for mine in (True, False):

            @pl.when((at == piece) & (own if mine else jnp.logical_not(own)))
            def _(ref=refs[2 * piece + (0 if mine else 1)]):
                value_ref[...] = ref[...].astype(f32)

    return value_ref[...]


def add_kernel(side_ref, rows_ref, *refs):
    refs[-2][...] = rows_ref[...] + pick_piece(side_ref, refs[:-2], refs[-1])


def add_pieces(rows, side, parts):
    count, width = rows.shape
    block = row_blocks(count)
    by_rows = pl.BlockSpec((block, width), lambda i, side: (i, 0))
    return call(
        add_kernel,
        jax.ShapeDtypeStruct(rows.shape, f32),
        (side, rows, *parts),
        [by_rows] + piece_specs(count, width, block),
        by_rows,
        grid=(count // block,),
        prefetch=1,
        scratch=(pltpu.VMEM((block, width), f32),),
    )


def middle_kernel(side_ref, rows_ref, gain_ref, *refs):
    middle_ref, low_ref, turned_ref, value_ref = refs[-4:]
    middle = rows_ref[...] + pick_piece(side_ref, refs[:-4], value_ref)
    middle_ref[...] = middle
    second = middle * inverse_norm(middle) * gain_ref[...]
    low_ref[...] = second.astype(bf)
    turned_ref[...] = second.T.astype(bf)


def turn_kernel(rows_ref, low_ref, turned_ref):
    rows = rows_ref[...]
    low_ref[...] = rows.astype(bf)
    turned_ref[...] = rows.T.astype(bf)


def round_and_turn(rows):
    count, width = rows.shape
    block = row_blocks(count)
    by_rows = pl.BlockSpec((block, width), lambda i: (i, 0))
    return call(
        turn_kernel,
        (jax.ShapeDtypeStruct(rows.shape, bf), jax.ShapeDtypeStruct((width, count), bf)),
        (rows,),
        [by_rows],
        (by_rows, pl.BlockSpec((width, block), lambda i: (0, i))),
        grid=(count // block,),
    )


def add_and_norm(rows, gain, side, parts):
    count, width = rows.shape
    block = row_blocks(count)
    by_rows = pl.BlockSpec((block, width), lambda i, side: (i, 0))
    whole = pl.BlockSpec((1, width), lambda i, side: (0, 0))
    return call(
        middle_kernel,
        (
            jax.ShapeDtypeStruct(rows.shape, f32),
            jax.ShapeDtypeStruct(rows.shape, bf),
            jax.ShapeDtypeStruct((width, count), bf),
        ),
        (side, rows, gain[None], *parts),
        [by_rows, whole] + piece_specs(count, width, block),
        (by_rows, by_rows, pl.BlockSpec((width, block), lambda i, side: (0, i))),
        grid=(count // block,),
        prefetch=1,
        scratch=(pltpu.VMEM((block, width), f32),),
    )


def back_rows(rows, gain_ref, base_ref, grad):
    inverse = inverse_norm(rows)
    normal = rows * inverse
    scaled = grad * gain_ref[...]
    out = base_ref[...] + inverse * (scaled - normal * jnp.mean(scaled * normal, axis=-1, keepdims=True))
    return out, grad * normal


def back_kernel(side_ref, rows_ref, gain_ref, base_ref, *refs):
    grad = pick_piece(side_ref, refs[:-2], refs[-1])
    refs[-2][...] = back_rows(rows_ref[...], gain_ref, base_ref, grad)[0]


def norm_back(rows, gain, base, side, parts):
    count, width = rows.shape
    block = row_blocks(count)
    by_rows = pl.BlockSpec((block, width), lambda i, side: (i, 0))
    whole = pl.BlockSpec((1, width), lambda i, side: (0, 0))
    return call(
        back_kernel,
        jax.ShapeDtypeStruct(rows.shape, f32),
        (side, rows, gain[None], base, *parts),
        [by_rows, whole, by_rows] + piece_specs(count, width, block),
        by_rows,
        grid=(count // block,),
        prefetch=1,
        scratch=(pltpu.VMEM((block, width), f32),),
    )


def back_project_kernel(side_ref, rows_ref, gain_ref, base_ref, mat_ref, *refs):
    out_ref, low_ref, project_ref, gain_out_ref, value_ref = refs[-5:]
    grad = pick_piece(side_ref, refs[:-5], value_ref)
    out, gain_terms = back_rows(rows_ref[...], gain_ref, base_ref, grad)
    low = out.astype(bf)
    out_ref[...] = out
    low_ref[...] = low
    project_ref[...] = product(low, mat_ref[:, mat_ref.shape[1] - project_ref.shape[1] :]).astype(bf)
    part = jnp.sum(gain_terms, axis=0, keepdims=True)

    @pl.when(pl.program_id(0) == 0)
    def _():
        gain_out_ref[...] = part

    @pl.when(pl.program_id(0) > 0)
    def _():
        gain_out_ref[...] += part


def norm_back_and_project(rows, gain, base, side, parts, mat, columns):
    count, width = rows.shape
    block = row_blocks(count)
    by_rows = pl.BlockSpec((block, width), lambda i, side: (i, 0))
    whole = pl.BlockSpec((1, width), lambda i, side: (0, 0))
    return call(
        back_project_kernel,
        (
            jax.ShapeDtypeStruct(rows.shape, f32),
            jax.ShapeDtypeStruct(rows.shape, bf),
            jax.ShapeDtypeStruct((count, columns), bf),
            jax.ShapeDtypeStruct((1, width), f32),
        ),
        (side, rows, gain[None], base, mat, *parts),
        [by_rows, whole, by_rows, pl.BlockSpec(mat.shape, lambda i, side: (0, 0))]
        + piece_specs(count, width, block),
        (by_rows, by_rows, pl.BlockSpec((block, columns), lambda i, side: (i, 0)), whole),
        grid=(count // block,),
        prefetch=1,
        scratch=(pltpu.VMEM((block, width), f32),),
    )


def pair_kernel(left_ref, right_ref, out_ref):
    out_ref[...] = (left_ref[...].astype(f32) + right_ref[...].astype(f32)).astype(bf)


def add_pair(left, right):
    count, width = left.shape
    block = count
    by_rows = pl.BlockSpec((block, width), lambda i: (i, 0))
    return call(
        pair_kernel,
        jax.ShapeDtypeStruct(left.shape, bf),
        (left, right),
        [by_rows, by_rows],
        by_rows,
        grid=(1,),
    )


def write_quarter(side_ref, quarter, value, refs):
    for own in (True, False):
        kept = side_ref[0] == quarter // PIECES

        @pl.when(kept if own else jnp.logical_not(kept))
        def _(ref=refs[quarter % PIECES + (0 if own else PIECES)]):
            ref[...] = value.astype(bf)


def quarter_shapes(rows, width):
    return (jax.ShapeDtypeStruct((rows // (2 * PIECES), width), bf),) * (2 * PIECES)


def probabilities(keys, queries, bias):
    shifted = against_rows(keys, queries) * HD ** (-0.5) + bias
    expo = jnp.exp(shifted - jnp.max(shifted, axis=0, keepdims=True))
    return expo * (1.0 / jnp.sum(expo, axis=0, keepdims=True))


def mask_bias(segment_col, segment_row, start, heads):
    shape = (segment_col.shape[0], segment_row.shape[1])
    key_at = lax.broadcasted_iota(jnp.int32, shape, 0)
    query_at = start + lax.broadcasted_iota(jnp.int32, shape, 1)
    allowed = (query_at >= key_at) & (segment_col == segment_row)
    return jnp.concatenate([jnp.where(allowed, 0.0, -1e30)] * heads, axis=1)


def heads_below(ref, here, heads):
    return jnp.concatenate([ref[here, h * HD : (h + 1) * HD] for h in range(heads)], axis=0)


def heads_beside(value, heads):
    size = value.shape[0] // heads
    return jnp.concatenate([value[h * size : (h + 1) * size] for h in range(heads)], axis=1)


def attend_kernel(heads, block, side_ref, qkv_ref, row_ref, col_ref, mat_ref, out_ref, *term_refs):
    keys_at = slice(heads * HD, (heads + 1) * HD)
    values_at = slice((heads + 1) * HD, (heads + 2) * HD)
    for start in range(0, qkv_ref.shape[0], block):
        here = slice(start, start + block)
        seen = slice(0, start + block)
        bias = mask_bias(col_ref[0, seen], row_ref[0, :, here], start, heads)
        probs = probabilities(qkv_ref[seen, keys_at], heads_below(qkv_ref, here, heads), bias)
        out = over_rows(qkv_ref[seen, values_at], probs.astype(bf))
        out = heads_beside(out.T.astype(bf), heads)
        out_ref[here] = out
        term = against_rows(out, mat_ref[:, (heads + 2) * HD :])
        write_quarter(side_ref, start // block, term, term_refs)


def attend_back_kernel(
    heads,
    block,
    side_ref,
    qkv_ref,
    row_ref,
    col_ref,
    mat_ref,
    grad_ref,
    rows_ref,
    out_ref,
    *refs,
):
    gain_ref, dk_ref, dv_ref = refs[-3:]
    scale = HD ** (-0.5)
    keys_at = slice(heads * HD, (heads + 1) * HD)
    values_at = slice((heads + 1) * HD, (heads + 2) * HD)
    rows = qkv_ref.shape[0]
    for start in range(rows - block, -1, -block):
        here = slice(start, start + block)
        seen = slice(0, start + block)
        bias = mask_bias(col_ref[0, seen], row_ref[0, :, here], start, heads)
        queries, grad = heads_below(qkv_ref, here, heads), heads_below(grad_ref, here, heads)
        probs = probabilities(qkv_ref[seen, keys_at], queries, bias)
        d_values = product(probs.astype(bf), grad)
        d_probs = against_rows(qkv_ref[seen, values_at], grad)
        d_scores = (probs * (d_probs - jnp.sum(probs * d_probs, axis=0, keepdims=True))).astype(bf)
        d_keys = product(d_scores, queries)
        if start == rows - block:
            dv_ref[...] = d_values
            dk_ref[...] = d_keys
        else:
            dv_ref[seen] += d_values
            dk_ref[seen] += d_keys
        d_queries = over_rows(qkv_ref[seen, keys_at], d_scores)
        out_ref[here, : heads * HD] = heads_beside((d_queries.T * scale).astype(bf), heads)
    out_ref[:, keys_at] = (dk_ref[...] * scale).astype(bf)
    out_ref[:, values_at] = dv_ref[...].astype(bf)
    gain = jnp.zeros(gain_ref.shape, f32)
    for start in range(0, rows, block):
        here = slice(start, start + block)
        first = against_rows(out_ref[here], mat_ref[:, : (heads + 2) * HD])
        write_quarter(side_ref, start // block, first, refs[:-3])
        inputs = rows_ref[here]
        gain += jnp.sum(first * (inputs * inverse_norm(inputs)), axis=0, keepdims=True)
    gain_ref[...] = gain


def attention(qkv, segments, heads, side, mat, grad=None, inputs=None):
    count, length = segments.shape
    assert count == 1
    rows, columns = qkv.shape
    width = mat.shape[0]
    block = length // (2 * PIECES)

    def whole(shape):
        return pl.BlockSpec(shape, lambda i, side: (0,) * len(shape))

    ins = (side, qkv, segments[:, None, :], segments[:, :, None], mat)
    if grad is not None:
        ins += (grad, inputs)
    in_specs = [whole(v.shape) for v in ins[1:]]
    quarters = quarter_shapes(rows, width)
    if grad is None:
        outs = (jax.ShapeDtypeStruct((rows, heads * HD), bf), *quarters)
    else:
        outs = (jax.ShapeDtypeStruct(qkv.shape, bf), *quarters, jax.ShapeDtypeStruct((1, width), f32))
    return call(
        partial(attend_kernel if grad is None else attend_back_kernel, heads, block),
        outs,
        ins,
        in_specs,
        tuple(whole(v.shape) for v in outs),
        grid=(1,),
        prefetch=1,
        scratch=() if grad is None else (pltpu.VMEM((length, HD), f32), pltpu.VMEM((length, HD), f32)),
    )


def attention_grads_kernel(own_rows, low_ref, d_qkv_ref, mid_ref, attended_ref, gain_ref, out_ref):
    split = d_qkv_ref.shape[1]
    left = over_rows(low_ref[...], d_qkv_ref[...]).astype(bf)
    right = over_rows(mid_ref[...], attended_ref[...]).astype(bf)
    for owner in range(out_ref.shape[0]):
        here = slice(owner * own_rows, (owner + 1) * own_rows)
        out_ref[owner, :own_rows, :split] = left[here]
        out_ref[owner, :own_rows, split:] = right[here]
        out_ref[owner, own_rows:] = gain_ref[owner]


def attention_grads(first_low, d_qkv, mid_low, attended, gain_rows, own_rows):
    rows, width = first_low.shape
    columns = d_qkv.shape[1] + attended.shape[1]
    block = width // 2
    owners = block // own_rows
    extra = gain_rows.shape[1]
    tile = pl.BlockSpec((rows, block), lambda j: (0, j))

    def whole(value):
        return pl.BlockSpec(value.shape, lambda j: (0, 0))

    def per(count):
        return pl.BlockSpec((owners, count, columns), lambda j: (j, 0, 0))

    return call(
        partial(attention_grads_kernel, own_rows),
        jax.ShapeDtypeStruct((width // own_rows, own_rows + extra, columns), bf),
        (first_low, d_qkv, mid_low, attended, gain_rows),
        [tile, whole(d_qkv), tile, whole(attended), per(extra)],
        per(own_rows + extra),
        grid=(width // block,),
    )


GELU_SLOPE = math.sqrt(2.0 / math.pi)
GELU_CUBE = 0.044715


def expert_kernel(pieces, first_expert, own_ff, at_ref, second_ref, grad_ref, routes_ref, gates_ref, *refs):
    sources = refs[: len(pieces)]
    hidden_ref, back_ref, mat_out_ref, mat_ref, come_ref, gone_ref = refs[len(pieces) :]
    rows, cols = hidden_ref.shape
    out = pltpu.make_async_copy(mat_ref, mat_out_ref, gone_ref.at[0])

    @pl.when(pl.program_id(0) == 0)
    def _():
        copies = []
        for k, count in enumerate(pieces):
            there = pl.ds(pl.multiple_of(at_ref[k], 16), count)
            copies.append(pltpu.make_async_copy(sources[k], mat_ref.at[there], come_ref.at[k]))
        for copy in copies:
            copy.start()
        for copy in copies:
            copy.wait()
        out.start()

    gate = product(second_ref[...], mat_ref[:, :cols])
    up = product(second_ref[...], mat_ref[:, cols : 2 * cols])
    d_hidden = product(grad_ref[...], mat_ref[:, 2 * cols :])
    routes, gates = routes_ref[...], gates_ref[...]
    of_col = lax.broadcasted_iota(jnp.int32, (rows, cols), 1) // own_ff
    combine = jnp.zeros((rows, cols), f32)
    for e in range(cols // own_ff):
        share = jnp.sum(jnp.where(routes == first_expert + e, gates, 0.0), axis=1, keepdims=True)
        combine = jnp.where(of_col == e, share, combine)
    square = gate * gate
    curve = jnp.tanh(GELU_SLOPE * gate * (1.0 + GELU_CUBE * square))
    half = 0.5 * (1.0 + curve)
    act = combine * (gate * half)
    slope = half + 0.5 * gate * (1.0 - curve * curve) * (GELU_SLOPE * (1.0 + 3.0 * GELU_CUBE * square))
    hidden_ref[...] = (act * up).astype(bf)
    back_ref[0] = (d_hidden * (combine * up * slope)).astype(bf)
    back_ref[1] = (d_hidden * act).astype(bf)

    @pl.when(pl.program_id(0) == pl.num_programs(0) - 1)
    def _():
        out.wait()


def experts(second_low, grad_low, ring, routes, gates, first_expert, own_ff):
    rows, width = second_low.shape
    cols = ring.columns // 3
    block = min(512, rows)
    at = jnp.stack([jnp.asarray(p[1], jnp.int32) for p in ring.pieces])
    arrays = [p[0] for p in ring.pieces]
    mat = jax.ShapeDtypeStruct((width, ring.columns), bf)

    def by_rows(size):
        return pl.BlockSpec((block, size), lambda i, at: (i, 0))

    return call(
        partial(expert_kernel, [a.shape[0] for a in arrays], first_expert, own_ff),
        (jax.ShapeDtypeStruct((rows, cols), bf), jax.ShapeDtypeStruct((2, rows, cols), bf), mat),
        (at, second_low, grad_low, routes, gates, *arrays),
        [by_rows(width), by_rows(width), by_rows(routes.shape[1]), by_rows(gates.shape[1])]
        + anywhere(len(arrays)),
        (by_rows(cols), pl.BlockSpec((2, block, cols), lambda i, at: (0, i, 0)), anywhere(1)[0]),
        grid=(rows // block,),
        prefetch=1,
        scratch=(
            pltpu.VMEM(mat.shape, bf),
            pltpu.SemaphoreType.DMA((len(arrays),)),
            pltpu.SemaphoreType.DMA((1,)),
        ),
    )


def against_mat(kind, hidden_ref, back_ref, mat_ref):
    cols = hidden_ref.shape[1]
    if kind == "hidden":
        return against_rows(hidden_ref[...], mat_ref[:, 2 * cols :])
    return against_rows(back_ref[0], mat_ref[:, :cols]) + against_rows(back_ref[1], mat_ref[:, cols : 2 * cols])


def group_kernel(hidden_ref, back_ref, mat_ref, term_ref, second_ref):
    term_ref[...] = against_mat("hidden", hidden_ref, back_ref, mat_ref).astype(bf)
    second_ref[...] = against_mat("back", hidden_ref, back_ref, mat_ref).astype(bf)


def group_products(hidden, back, mat):
    rows = hidden.shape[0]
    width = mat.shape[0]
    block = min(512, width)
    out = jax.ShapeDtypeStruct((rows, width), bf)
    spec = pl.BlockSpec((rows, block), lambda j: (0, j))
    return call(
        group_kernel,
        (out, out),
        (hidden, back, mat),
        [
            pl.BlockSpec(hidden.shape, lambda j: (0, 0)),
            pl.BlockSpec(back.shape, lambda j: (0, 0, 0)),
            pl.BlockSpec((block, mat.shape[1]), lambda j: (j, 0)),
        ],
        (spec, spec),
        grid=(width // block,),
    )


def last_kernel(kind, side_ref, hidden_ref, back_ref, mat_ref, before_ref, *refs):
    value = against_mat(kind, hidden_ref, back_ref, mat_ref) + before_ref[...].astype(f32)
    size = refs[0].shape[0]
    for quarter in range(2 * PIECES):
        write_quarter(side_ref, quarter, value[quarter * size : (quarter + 1) * size], refs)


def last_product(kind, hidden, back, mat, before, side):
    rows = hidden.shape[0]
    width = mat.shape[0]
    block = min(512, width)
    shapes = quarter_shapes(rows, width)
    spec = pl.BlockSpec((shapes[0].shape[0], block), lambda j, side: (0, j))
    return call(
        partial(last_kernel, kind),
        shapes,
        (side, hidden, back, mat, before),
        [
            pl.BlockSpec(hidden.shape, lambda j, side: (0, 0)),
            pl.BlockSpec(back.shape, lambda j, side: (0, 0, 0)),
            pl.BlockSpec((block, mat.shape[1]), lambda j, side: (j, 0)),
            pl.BlockSpec((rows, block), lambda j, side: (0, j)),
        ],
        (spec,) * len(shapes),
        grid=(width // block,),
        prefetch=1,
    )


def expert_grads_kernel(second_ref, grad_ref, hidden_ref, back_ref, out_ref):
    cols = hidden_ref.shape[1]
    out_ref[:, :cols] = product(second_ref[...], back_ref[0]).astype(bf)
    out_ref[:, cols : 2 * cols] = product(second_ref[...], back_ref[1]).astype(bf)
    out_ref[:, 2 * cols :] = product(grad_ref[...], hidden_ref[...]).astype(bf)


def expert_grads(second_turned, grad_turned, hidden, back):
    width, rows = second_turned.shape
    cols = hidden.shape[1]
    block = min(512, width)
    tile = pl.BlockSpec((block, rows), lambda j: (j, 0))
    return call(
        expert_grads_kernel,
        jax.ShapeDtypeStruct((width, 3 * cols), bf),
        (second_turned, grad_turned, hidden, back),
        [
            tile,
            tile,
            pl.BlockSpec(hidden.shape, lambda j: (0, 0)),
            pl.BlockSpec(back.shape, lambda j: (0, 0, 0)),
        ],
        pl.BlockSpec((block, 3 * cols), lambda j: (j, 0)),
        grid=(width // block,),
    )


def ring_member(place, n):
    place = place % n
    if n % 2:
        return place
    if isinstance(place, int):
        return 2 * place if place < n // 2 else 2 * n - 1 - 2 * place
    return jnp.where(place < n // 2, 2 * place, 2 * n - 1 - 2 * place)


def ring_place(index, n):
    if n % 2:
        return index
    return jnp.where(index % 2 == 0, index // 2, n - 1 - index // 2)


def ring_sides(n):
    members = [ring_member(p, n) for p in range(n)]
    up = [(members[p], members[(p + 1) % n]) for p in range(n)]
    down = [(members[(p + 1) % n], members[p]) for p in range(n)]
    return up, down


class RingGather:
    def __init__(self, block, rows, far_up):
        self.n = lax.axis_size("dp")
        self.rows, self.columns = rows, block.shape[1]
        self.extra = block.shape[0] - rows
        self.far_up = far_up
        self.place = ring_place(lax.axis_index("dp"), self.n)
        self.up, self.down = ring_sides(self.n)
        self.reach = self.n // 2
        self.arrived = self.stage = 0
        self.buffers = None
        self.pieces = [(block, ring_member(self.place, self.n) * rows)]
        self.send(block, block)

    def send(self, low, high):
        last = self.arrived == self.reach - 1
        self.low = lax.ppermute(low, "dp", self.up) if self.far_up or not last else None
        self.high = lax.ppermute(high, "dp", self.down) if not (self.far_up and last) else None

    def put(self, arrays, members):
        arrays = [*arrays, None]
        self.buffers = put(self.buffers, arrays[0], arrays[1], self.rows, self.extra, members)

    def put_pieces(self):
        self.buffers = [unwritten((self.n * self.rows, self.columns), bf)]
        if self.extra:
            self.buffers.append(unwritten((self.n * self.extra, self.columns), bf))
        self.put([self.pieces[0][0]], [ring_member(self.place, self.n)])

    def receive(self):
        self.stage += 1
        upto = self.reach if self.stage == 4 else (self.reach - 1) * self.stage // 3
        while self.arrived < upto:
            came = after(*(v for v in (self.low, self.high) if v is not None))
            self.arrived += 1
            members = [
                ring_member(self.place - self.arrived + self.n, self.n),
                ring_member(self.place + self.arrived, self.n),
            ][: len(came)]
            if self.arrived < self.reach:
                self.send(*came)
            self.pieces += [(value, member * self.rows) for value, member in zip(came, members)]
            if self.buffers:
                self.put(came, members)


def step_kernel(near_ref, at_ref, up_ref, down_ref, *refs):
    def add(left, right):
        return (left.astype(f32) + right.astype(f32)).astype(bf)

    got = refs[:-2]
    for k, (mine_ref, sum_ref) in enumerate(((up_ref, refs[-2]), (down_ref, refs[-1]))):
        if near_ref is None:
            sum_ref[...] = add(mine_ref[...], got[k][...])
        elif near_ref == k:
            sum_ref[...] = mine_ref[...]
        else:
            sum_ref[...] = add(mine_ref[...], got[0][...])


def copy_kernel(at_ref, from_ref, to_ref):
    to_ref[...] = from_ref[...]


class RingScatter:
    def __init__(self, total, far_up):
        self.total = total
        self.n = lax.axis_size("dp")
        self.rows = total.shape[0] // self.n
        self.reach = self.n // 2
        self.hop = self.reach
        self.stage = 0
        self.far_up = far_up
        self.place = ring_place(lax.axis_index("dp"), self.n)
        self.up, self.down = ring_sides(self.n)
        far = self.far()
        self.to_high = lax.ppermute(far, "dp", self.up) if far_up else None
        self.to_low = None if far_up else lax.ppermute(far, "dp", self.down)

    def block(self, steps=1, k=0):
        shape = (self.rows // steps, self.total.shape[1])
        return pl.BlockSpec(shape, lambda i, at: (at[k] * steps + i, 0))

    def far(self):
        shape = (self.rows, self.total.shape[1])
        at = ring_member(self.place + self.reach, self.n).astype(jnp.int32)[None]
        return call(
            copy_kernel,
            jax.ShapeDtypeStruct(shape, bf),
            (at, self.total),
            [self.block()],
            pl.BlockSpec(shape, lambda i, at: (0, 0)),
            grid=(1,),
            prefetch=1,
        )

    def take(self, at):
        return lax.dynamic_slice_in_dim(self.total, ring_member(at, self.n) * self.rows, self.rows, 0)

    def step(self):
        self.stage += 1
        columns = self.total.shape[1]
        while self.hop > self.reach - (self.reach - 1) * self.stage // 3:
            near = (1 if self.far_up else 0) if self.hop == self.reach else None
            self.hop -= 1
            at = jnp.stack(
                [
                    ring_member(self.place + self.hop, self.n),
                    ring_member(self.place - self.hop + self.n, self.n),
                ]
            ).astype(jnp.int32)
            steps = 1
            along = pl.BlockSpec((self.rows // steps, columns), lambda i, at: (i, 0))
            got = [v for v in (self.to_high, self.to_low) if v is not None]
            out = jax.ShapeDtypeStruct((self.rows, columns), bf)
            sums = call(
                partial(step_kernel, near),
                (out, out),
                (at, self.total, self.total, *got),
                [self.block(steps, 0), self.block(steps, 1)] + [along] * len(got),
                (along, along),
                grid=(steps,),
                prefetch=1,
            )
            self.to_high = lax.ppermute(sums[0], "dp", self.up)
            self.to_low = lax.ppermute(sums[1], "dp", self.down)

    def close(self):
        self.to_high, self.to_low = after(self.to_high, self.to_low)

    def finish(self):
        self.close()
        mine = self.take(self.place).astype(f32)
        return mine + self.to_high.astype(f32) + self.to_low.astype(f32)


def swap_along_tensor(value, bit):
    n = lax.axis_size("tensor")
    return lax.ppermute(value, "tensor", [(t, t ^ bit) for t in range(n)])


class TensorSum:
    def __init__(self, quarters):
        self.kept = quarters[:PIECES]
        self.got = [swap_along_tensor(sent, 1) for sent in quarters[PIECES:]]
        self.here, self.there, self.parts = {}, {}, []

    def across(self, *pieces):
        for piece in pieces or range(PIECES):
            self.here[piece] = add_pair(self.kept[piece], self.got[piece])
            self.there[piece] = swap_along_tensor(self.here[piece], 2)

    def back(self, *pieces):
        for piece in pieces or range(PIECES):
            total = add_pair(self.here[piece], self.there[piece])
            self.parts += [total, swap_along_tensor(total, 1)]


def keyval_scatter(part, gains):
    t = lax.axis_index("tensor")
    core, side = t % 2, t // 2
    rows = part.shape[0] // 4

    def quarter(index):
        return lax.dynamic_slice_in_dim(part, index * rows, rows, 0)

    gains = jnp.pad(gains, ((0, 6), (0, 2 * HD - gains.shape[1])))
    got = swap_along_tensor(jnp.concatenate([quarter(1 - core), quarter(3 - core), gains]), 1)
    mine = jnp.concatenate([quarter(core), quarter(core + 2), gains]) + got
    kept = jnp.where(side == 0, mine[:rows], mine[rows : 2 * rows])
    leaving = jnp.where(side == 0, mine[rows : 2 * rows], mine[:rows])
    other = swap_along_tensor(jnp.concatenate([leaving, mine[2 * rows :]]), 2)
    gains = (mine[2 * rows :] + other[rows:])[:2]
    other = other[:rows]
    heads = [jnp.where(side == 0, kept, other), jnp.where(side == 0, other, kept)]
    sums = jnp.concatenate([h[:, :HD] for h in heads] + [h[:, HD:] for h in heads], axis=1)
    return sums, gains


def body(
    block_input,
    segments,
    routes,
    gates,
    cotangent,
    w_query,
    m_query,
    v_query,
    w_keyval,
    m_keyval,
    v_keyval,
    w_output,
    m_output,
    v_output,
    w_gate_up,
    m_gate_up,
    v_gate_up,
    w_down,
    m_down,
    v_down,
    gains,
    m_gains,
    v_gains,
):
    ORDER.clear()
    width = block_input.shape[1]
    tensors = lax.axis_size("tensor")
    heads_here = H // tensors
    t = lax.axis_index("tensor")
    kv_head = t * heads_here // (H // KVH)
    side = (t % 2).astype(jnp.int32)[None]
    own_rows = w_query.shape[0]
    head_cols = heads_here * HD
    own_ff = w_gate_up.shape[3]
    kv_cols = 2 * KVH * HD
    own_gain = gains.shape[1]

    own_kv = w_keyval.reshape(w_keyval.shape[0], -1).astype(bf)
    terms, left = [], gains
    for _ in range(3):
        term = lax.reduce_precision(left, 8, 7)
        left = left - term
        terms.append(term.astype(bf))
    own_terms = jnp.pad(jnp.concatenate(terms, axis=0), ((0, 10), (0, kv_cols - own_gain)))
    small = jnp.concatenate([own_kv, own_terms], axis=0)[None]
    for bit in (1, 2):
        other = swap_along_tensor(small, bit)
        upper = (t // bit) % 2
        small = jnp.where(
            upper == 0, jnp.concatenate([small, other]), jnp.concatenate([other, small])
        )
    kv_rows = small[:, : own_kv.shape[0]].reshape(own_rows, kv_cols)
    gain_block = small[:, own_kv.shape[0] :, :own_gain].transpose(1, 0, 2).reshape(16, tensors * own_gain)
    attn_cols = 2 * head_cols + 2 * HD
    attn_block = jnp.concatenate(
        [
            jnp.concatenate(
                [
                    w_query.astype(bf),
                    lax.dynamic_slice_in_dim(kv_rows, kv_head * HD, HD, 1),
                    lax.dynamic_slice_in_dim(kv_rows, (KVH + kv_head) * HD, HD, 1),
                    w_output.T.astype(bf),
                ],
                axis=1,
            ),
            jnp.pad(gain_block, ((0, 0), (0, attn_cols - tensors * own_gain))),
        ],
        axis=0,
    )
    qkv_cols = head_cols + 2 * HD
    in_group = E // 2
    cols = in_group * own_ff
    gate_up_low = w_gate_up.astype(bf).reshape(own_rows, 2 * E * own_ff)
    down_low = w_down.astype(bf).transpose(2, 0, 1).reshape(own_rows, E * own_ff)
    blocks = [
        jnp.concatenate(
            [
                gate_up_low[:, g * cols : (g + 1) * cols],
                gate_up_low[:, (2 + g) * cols : (3 + g) * cols],
                down_low[:, g * cols : (g + 1) * cols],
            ],
            axis=1,
        )
        for g in range(2)
    ]

    attn_ring = RingGather(attn_block, own_rows, True)
    attn_ring.put_pieces()
    blocks[:1] = after(blocks[0])
    attn_ring.receive()
    blocks[1:] = after(blocks[1])
    attn_ring.receive()
    attn_ring.receive()
    ring_0 = RingGather(blocks[0], own_rows, False)
    attn_ring.receive()
    attn_mat, gain_rest = attn_ring.buffers
    gain_terms = gain_rest.reshape(-1, 16, attn_cols)[:, :6, : tensors * own_gain].astype(f32)
    gain_rows = gain_terms[:, 0:2] + gain_terms[:, 2:4] + gain_terms[:, 4:6]
    gain_rows = gain_rows.transpose(1, 0, 2).reshape(2, width)

    first_low, qkv = norm_and_project(block_input, gain_rows[0], attn_mat, qkv_cols)
    ring_0.receive()
    attended, *quarters = attention(qkv, segments, heads_here, side, attn_mat)
    attn_sum = TensorSum(quarters)
    attn_sum.across()
    ring_0.receive()
    grad_low, grad_turned = round_and_turn(cotangent)
    ring_0.receive()
    ring_1 = RingGather(blocks[1], own_rows, True)
    attn_sum.back()
    ring_0.receive()
    middle, second_low, second_turned = add_and_norm(block_input, gain_rows[1], side, attn_sum.parts)
    ring_1.receive()
    hidden_0, back_0, mat_0 = experts(second_low, grad_low, ring_0, routes, gates, 0, own_ff)
    ring_1.receive()
    scatter_0 = RingScatter(expert_grads(second_turned, grad_turned, hidden_0, back_0), True)
    ring_1.receive()
    term_0, second_0 = group_products(hidden_0, back_0, mat_0)
    ring_1.receive()
    hidden_1, back_1, mat_1 = experts(second_low, grad_low, ring_1, routes, gates, in_group, own_ff)
    scatter_0.step()
    second_sum = TensorSum(last_product("back", hidden_1, back_1, mat_1, second_0, side))
    second_sum.across()
    scatter_0.step()
    scatter_1 = RingScatter(expert_grads(second_turned, grad_turned, hidden_1, back_1), False)
    scatter_0.step()
    expert_sum = TensorSum(last_product("hidden", hidden_1, back_1, mat_1, term_0, side))
    second_sum.back()
    scatter_1.step()
    expert_sum.across(0)
    d_middle, mid_low, d_attended, gain_two = norm_back_and_project(
        middle, gain_rows[1], cotangent, side, second_sum.parts, attn_mat, head_cols
    )
    scatter_0.close()
    scatter_1.step()
    expert_sum.back(0)
    expert_sum.across(1)
    d_qkv, *quarters, gain_one = attention(
        qkv, segments, heads_here, side, attn_mat, d_attended, block_input
    )
    first_sum = TensorSum(quarters)
    scatter_1.step()
    expert_sum.back(1)
    first_sum.across()
    gain_parts = jnp.concatenate([gain_one, gain_two * (1.0 / tensors)], axis=0)
    gain_parts = gain_parts.reshape(2, -1, own_rows).transpose(1, 0, 2).astype(bf)
    gain_parts = jnp.pad(gain_parts, ((0, 0), (0, 14), (0, attn_cols - own_rows)))
    d_attn = attention_grads(first_low, d_qkv, mid_low, attended, gain_parts, own_rows)
    attn_scatter = RingScatter(d_attn.reshape(-1, attn_cols), True)
    block_output = add_pieces(middle, side, expert_sum.parts)
    attn_scatter.step()
    scatter_1.close()
    first_sum.back()
    attn_scatter.step()
    input_grad = norm_back(block_input, gain_rows[0], d_middle, side, first_sum.parts)
    attn_scatter.step()
    sums = [scatter_0.finish(), scatter_1.finish()]
    sum_gate_up = jnp.concatenate(
        [s[:, part * cols : (part + 1) * cols] for part in range(2) for s in sums], axis=1
    ).reshape(w_gate_up.shape)
    sum_down = jnp.concatenate([s[:, 2 * cols :] for s in sums], axis=1)
    sum_down = sum_down.reshape(own_rows, E, own_ff).transpose(1, 2, 0)
    sum_attn = attn_scatter.finish()
    sum_query = sum_attn[:own_rows, :head_cols]
    sum_output_t = sum_attn[:own_rows, qkv_cols:]
    sum_keyval, sum_gains = keyval_scatter(
        sum_attn[:own_rows, head_cols:qkv_cols], sum_attn[own_rows : own_rows + 2, :own_rows]
    )
    sum_keyval = sum_keyval.reshape(w_keyval.shape)
    sum_gains = lax.dynamic_slice_in_dim(sum_gains, t * own_gain, own_gain, 1)
    query_new = adam_step(w_query, m_query, v_query, sum_query, 0.05, 0.1)
    keyval_new = adam_step(w_keyval, m_keyval, v_keyval, sum_keyval, 0.05, 0.1)
    output_new = adam_step(w_output, m_output, v_output, sum_output_t.T, 0.05, 0.1)
    gate_up_new = adam_step(w_gate_up, m_gate_up, v_gate_up, sum_gate_up, 0.05, 0.1)
    down_new = adam_step(w_down, m_down, v_down, sum_down, 0.05, 0.1)
    gains_new = adam_step(gains, m_gains, v_gains, sum_gains, 0.5, 0.0)
    return (
        block_output,
        input_grad,
        *query_new,
        *keyval_new,
        *output_new,
        *gate_up_new,
        *down_new,
        *gains_new,
    )


def solution(mesh):
    states = [
        P("dp", "tensor"),
        P(("dp", "tensor"), None, None),
        P("tensor", "dp"),
        P("dp", None, None, "tensor"),
        P(None, "tensor", "dp"),
        P(None, ("dp", "tensor")),
    ]
    placed = (P("dp", None),) * 5 + tuple(s for s in states for _ in range(3))
    return jax.shard_map(
        body,
        mesh=mesh,
        in_specs=placed,
        out_specs=(P("dp", None),) * 2 + tuple(s for s in states for _ in range(3)),
        check_vma=False,
    )
```
